32 devices in a mesh: ctx: 4 (over z), head: 8 (over y, x, core).
Axes of the slice: x: 2, y: 2, z: 4, core: 2. Of those that a mesh axis runs over, the one named last changes fastest.
Arguments:
- queries: bfloat16 [2048, 2048], P('ctx', 'head'), may hold values from -24 to 24, as said below
- keys: bfloat16 [2048, 256], P('ctx'), may hold values from -24 to 24
- values: bfloat16 [2048, 256], P('ctx'), may hold values from -6 to 6
- out_grad: bfloat16 [2048, 2048], P('ctx', 'head'), may hold values from -6 to 6
- doc_start: int32 [2048], P('ctx'), may hold values from 0 to 2047, as said below
Outputs:
- attn_out: bfloat16 [2048, 2048], P('ctx', 'head')
- query_grad: bfloat16 [2048, 2048], P('ctx', 'head')
- key_grad: float32 [2048, 256], P('ctx', 'head')
- value_grad: float32 [2048, 256], P('ctx', 'head')
The draws below stay inside these ranges and needn't reach their ends.
Inputs may be any that keep to these rules, and one draw needn't show every extreme that they name: Query and key entries lie within the range; in some draws a few queries are close to multiples of visible keys. doc_start[0] = 0; for i > 0 either doc_start[i] = i (a document begins) or doc_start[i] = doc_start[i - 1]. Documents may cross device boundaries. The last token begins a document of its own.
All inputs are finite; a program needn't handle non-finite values.
Results may differ from the reference program's by a relative error of at most 0.019.
Values may be sent and summed in bfloat16 or wider, within the bound.
No kernel may reach another device: no remote copies, remote signals or barrier semaphores. Data moves between devices by JAX's collectives and lax.ppermute only.
A program may use at most 64 MiB of HBM per device.

```python
import math
import jax
import jax.numpy as jnp
from jax import lax

HEAD_DIM = 128
QUERY_HEADS = 16
KV_HEADS = 2
WINDOW = 1024
TOKENS = 2048


def query_key_pair(key):
    base_key = jax.random.fold_in(key, 7331)
    first, second = jax.random.split(base_key, 2)
    per_group = QUERY_HEADS // KV_HEADS
    query_draw = jax.random.normal(first, (TOKENS, KV_HEADS, per_group, HEAD_DIM), jnp.float32)
    key_draw = jax.random.normal(second, (TOKENS, KV_HEADS, HEAD_DIM), jnp.float32)
    query_draw = jnp.clip(query_draw, -6.0, 6.0)
    key_draw = jnp.clip(key_draw, -6.0, 6.0)
    query_draw = jnp.clip(query_draw, -24.0, 24.0)
    key_draw = jnp.clip(key_draw, -24.0, 24.0)
    return (query_draw.reshape(TOKENS, QUERY_HEADS * HEAD_DIM), key_draw.reshape(TOKENS, KV_HEADS * HEAD_DIM))


def draw_queries(key, part):
    return query_key_pair(key)[0].astype(jnp.bfloat16)


def draw_keys(key, part):
    return query_key_pair(key)[1].astype(jnp.bfloat16)


def draw_doc_start(key, part):
    ticket = jax.random.randint(jax.random.fold_in(key, 4242), (TOKENS,), 0, 2 * WINDOW)
    forced = jax.random.randint(jax.random.fold_in(key, 4343), (), TOKENS // 4, 3 * TOKENS // 4)
    position = jnp.arange(TOKENS, dtype=jnp.int32)
    begins = (ticket < 1) | (position == 0) | (position == TOKENS - 1) | (position == forced)
    marked = jnp.where(begins, position, 0).astype(jnp.int32)
    return lax.cummax(marked, axis=0).astype(jnp.int32)


def level_of(own_key, extent, pieces, low, top_value):
    def one(axis_at, blocks):
        heights = jax.random.uniform(jax.random.fold_in(jax.random.fold_in(own_key, 6), axis_at), (blocks,), jnp.float32, low / len(pieces), top_value / len(pieces))
        return jnp.repeat(jnp.exp(heights), extent[axis_at] // blocks).reshape((-1,) + (1,) * (len(extent) - axis_at - 1))

    factor_of = one(*pieces[0])
    for cut in pieces[1:]:
        factor_of = factor_of * one(*cut)
    return factor_of


def scatter_about(key, dims, deviation, most, shards=(), kind=jnp.bfloat16):
    result = deviation * jax.random.normal(key, dims, jnp.float32)
    if shards:
        result = result * level_of(key, dims, shards, -0.22, 0.18)
    return jnp.clip(result, -most, most).astype(kind)


def setup_inputs(seed: int = 0) -> dict:
    streams_of = jax.random.split(jax.random.key(seed), 6)
    queries = draw_queries(jax.random.fold_in(streams_of[5], 71), 0)
    keys = draw_keys(jax.random.fold_in(streams_of[5], 71), 0)
    values = scatter_about(streams_of[2], (TOKENS, KV_HEADS * HEAD_DIM), 1.0, 6.0, ((0, 4),))
    out_grad = scatter_about(streams_of[3], (TOKENS, QUERY_HEADS * HEAD_DIM), 1.0, 6.0, ((0, 4), (1, 8)))
    doc_start = draw_doc_start(jax.random.fold_in(streams_of[5], 71), 0)
    return {"queries": queries, "keys": keys, "values": values, "out_grad": out_grad, "doc_start": doc_start}


def reference(queries, keys, values, out_grad, doc_start):
    per_group = QUERY_HEADS // KV_HEADS
    block_rows = math.gcd(TOKENS, 512)
    score_scale = HEAD_DIM ** -0.5
    query_heads = queries.reshape(TOKENS, KV_HEADS, per_group, HEAD_DIM)
    grad_heads = out_grad.reshape(TOKENS, KV_HEADS, per_group, HEAD_DIM)
    padding = jnp.zeros((WINDOW, KV_HEADS, HEAD_DIM), keys.dtype)
    key_pad = jnp.concatenate([padding, keys.reshape(TOKENS, KV_HEADS, HEAD_DIM)], axis=0)
    value_pad = jnp.concatenate([padding, values.reshape(TOKENS, KV_HEADS, HEAD_DIM)], axis=0)

    def one_block(carry, row_start):
        key_acc, value_acc = carry
        query_block = lax.dynamic_slice_in_dim(query_heads, row_start, block_rows, 0).astype(jnp.float32)
        grad_block = lax.dynamic_slice_in_dim(grad_heads, row_start, block_rows, 0).astype(jnp.float32)
        key_block = lax.dynamic_slice_in_dim(key_pad, row_start, block_rows + WINDOW, 0).astype(jnp.float32)
        value_block = lax.dynamic_slice_in_dim(value_pad, row_start, block_rows + WINDOW, 0).astype(jnp.float32)
        starts = lax.dynamic_slice_in_dim(doc_start, row_start, block_rows, 0)
        query_pos = row_start + jnp.arange(block_rows, dtype=jnp.int32)
        key_pos = row_start - WINDOW + jnp.arange(block_rows + WINDOW, dtype=jnp.int32)
        visible = (key_pos[None, :] <= query_pos[:, None]) & (key_pos[None, :] > query_pos[:, None] - WINDOW) & (key_pos[None, :] >= starts[:, None])
        scores = jnp.einsum("qhgd,khd->hgqk", query_block, key_block) * score_scale
        masked = jnp.where(visible[None, None], scores, -1e30)
        row_max = jnp.max(masked, axis=-1, keepdims=True)
        weights = jnp.where(visible[None, None], jnp.exp(masked - row_max), 0.0)
        prob_full = weights / jnp.sum(weights, axis=-1, keepdims=True)
        prob_round = prob_full.astype(jnp.bfloat16).astype(jnp.float32)
        attended = jnp.einsum("hgqk,khd->qhgd", prob_round, value_block).astype(jnp.bfloat16)
        dprob = jnp.einsum("qhgd,khd->hgqk", grad_block, value_block)
        row_delta = jnp.transpose(jnp.sum(grad_block * attended.astype(jnp.float32), axis=-1), (1, 2, 0))
        dscore = (prob_full * (dprob - row_delta[..., None])).astype(jnp.bfloat16).astype(jnp.float32)
        q_grad = (jnp.einsum("hgqk,khd->qhgd", dscore, key_block) * score_scale).astype(jnp.bfloat16)
        key_part = jnp.einsum("hgqk,qhgd->khd", dscore, query_block) * score_scale
        value_part = jnp.einsum("hgqk,qhgd->khd", prob_round, grad_block)
        key_now = lax.dynamic_slice_in_dim(key_acc, row_start, block_rows + WINDOW, 0) + key_part
        value_now = lax.dynamic_slice_in_dim(value_acc, row_start, block_rows + WINDOW, 0) + value_part
        key_acc = lax.dynamic_update_slice_in_dim(key_acc, key_now, row_start, 0)
        value_acc = lax.dynamic_update_slice_in_dim(value_acc, value_now, row_start, 0)
        return (key_acc, value_acc), (attended, q_grad)

    block_starts = jnp.arange(TOKENS // block_rows, dtype=jnp.int32) * block_rows
    zero_acc = jnp.zeros((TOKENS + WINDOW, KV_HEADS, HEAD_DIM), jnp.float32)
    (key_acc, value_acc), (attended, q_grad) = lax.scan(one_block, (zero_acc, zero_acc), block_starts)
    attn_out = attended.reshape(TOKENS, QUERY_HEADS * HEAD_DIM)
    query_grad = q_grad.reshape(TOKENS, QUERY_HEADS * HEAD_DIM)
    key_grad = key_acc[WINDOW:].reshape(TOKENS, KV_HEADS * HEAD_DIM)
    value_grad = value_acc[WINDOW:].reshape(TOKENS, KV_HEADS * HEAD_DIM)
    return attn_out, query_grad, key_grad, value_grad
```

```python
import functools
import math

import jax
import jax.numpy as jnp
from jax import lax
from jax.experimental import pallas as pl
from jax.experimental.pallas import tpu as pltpu
from jax.sharding import PartitionSpec as P

HEAD_DIM = 128
WINDOW = 1024
GROUP = 4
SCALE = HEAD_DIM**-0.5
EXP2_SCALE = SCALE * math.log2(math.e)
HIDDEN = -1e30
SAFE_SUM = 2.0**64
F32 = jnp.float32
BF16 = jnp.bfloat16

NN = (((1,), (0,)), ((), ()))
NT = (((1,), (1,)), ((), ()))


def dot(a, b, dims):
    return lax.dot_general(a, b, dims, preferred_element_type=F32)


def tile_of(tok):
    return min(256, tok)


def col_blocks(tok, heads):
    tile = tile_of(tok)
    return [
        (t * tile, h, (t * heads + h) * tile) for t in range(tok // tile) for h in range(heads)
    ]


def wide_blocks(tok, heads):
    tile = tile_of(tok)
    return [(t * tile, slice(t * heads * tile, (t + 1) * heads * tile)) for t in range(tok // tile)]


def place_of(q0, h, tile):
    return slice(q0, q0 + tile), slice(h * HEAD_DIM, (h + 1) * HEAD_DIM)


def first_visible(doc_ref, q0, tile):
    start = lax.axis_index("ctx") * doc_ref.shape[1]
    query = q0 + lax.broadcasted_iota(jnp.int32, (1, tile), 1)
    return jnp.maximum(doc_ref[:, q0 : q0 + tile] - start, query - (WINDOW - 1))


def with_ones(vt):
    return jnp.concatenate([vt, jnp.ones((16, vt.shape[1]), BF16)], axis=0)


def weigh(vt_ones, eb):
    both = dot(vt_ones, eb, NN)
    return both[:HEAD_DIM], both[HEAD_DIM : HEAD_DIM + 1]


def pack_kernel(keys_hbm, values_hbm, half_ref, quarter_ref, sems):
    last = lax.axis_size("ctx") - 1
    head = lax.axis_index("head")
    tok = half_ref.shape[0]
    lanes = pl.ds(pl.multiple_of(head // GROUP * HEAD_DIM, HEAD_DIM), HEAD_DIM)
    rows = pl.ds(pl.multiple_of(head // 2 % 2 * (tok // 2), tok // 2), tok // 2)
    for odd, source in enumerate((keys_hbm, values_hbm)):

        @pl.when((lax.axis_index("ctx") + 2 <= last) & (head % 2 == odd))
        def _():
            copies = [
                pltpu.make_async_copy(source.at[rows, lanes], quarter_ref, sems.at[0]),
                pltpu.make_async_copy(source.at[:, lanes], half_ref, sems.at[1]),
            ]
            for copy in copies:
                copy.start()
            for copy in copies:
                copy.wait()


def late_pack_kernel(keys_hbm, values_hbm, _, half_ref, sem):
    last = lax.axis_size("ctx") - 1
    head = lax.axis_index("head")
    lanes = pl.ds(pl.multiple_of(head // GROUP * HEAD_DIM, HEAD_DIM), HEAD_DIM)
    for odd, source in enumerate((keys_hbm, values_hbm)):

        @pl.when((lax.axis_index("ctx") + 1 == last) & (head % 2 == odd))
        def _():
            copy = pltpu.make_async_copy(source.at[:, lanes], half_ref, sem)
            copy.start()
            copy.wait()


def beside_ones(rows):
    return jnp.concatenate([rows, jnp.ones((rows.shape[0], HEAD_DIM), BF16)], axis=1)


def less(columns, row):
    high = row.astype(BF16).astype(F32)
    middle = (row - high).astype(BF16).astype(F32)
    low = row - high - middle
    which = lax.broadcasted_iota(jnp.int32, (16, row.shape[1]), 0)
    block = jnp.where(which == 0, high, jnp.where(which == 1, middle, low))
    block = jnp.where(which < 3, -block, 0.0).astype(BF16)
    rest = jnp.zeros((HEAD_DIM - 16, row.shape[1]), BF16)
    return jnp.concatenate([columns, block, rest], axis=0)


def causal_kernel(bias_ref):
    key = lax.broadcasted_iota(jnp.int32, bias_ref.shape, 0)
    query = lax.broadcasted_iota(jnp.int32, bias_ref.shape, 1)
    bias_ref[...] = jnp.where(key <= query, 0.0, HIDDEN)


def own_kernel(
    tok, heads, causal_ref, doc_ref, q_ref, keys_ref, do_ref, values_ref,
    e_ref, dp_ref, o_ref, stat_ref, qt_ref, dot_ref, kt_ref, s_ref,
):
    tile = tile_of(tok)
    group = lax.axis_index("head") // GROUP
    lanes = pl.ds(pl.multiple_of(group * HEAD_DIM, HEAD_DIM), HEAD_DIM)
    k = keys_ref[:, lanes]
    v = values_ref[:, lanes]
    for q0, h, c0 in col_blocks(tok, heads):
        place = place_of(q0, h, tile)
        qt_ref[:, c0 : c0 + tile] = q_ref[place].T
        dot_ref[:, c0 : c0 + tile] = do_ref[place].T
    wide = wide_blocks(tok, heads)
    for q0, cols in wide:
        rows = q0 + tile
        first = first_visible(doc_ref, q0, tile)
        key = lax.broadcasted_iota(jnp.int32, (tile, tile), 0)
        bias = [jnp.where(key + r0 >= first, 0.0, HIDDEN) for r0 in range(0, q0, tile)]
        bias.append(jnp.where(key + q0 >= first, causal_ref[...], HIDDEN))
        bias = jnp.concatenate(bias, axis=0)
        s = dot(k[:rows], qt_ref[:, cols], NN) + jnp.concatenate([bias] * heads, axis=1)
        s_ref[0:rows, cols] = s
        stat_ref[0:1, cols] = jnp.max(s, axis=0, keepdims=True)
    kt_ref[...] = k.T
    vt = with_ones(v.T)
    for q0, cols in wide:
        rows = q0 + tile
        eb = jnp.exp2((s_ref[0:rows, cols] - stat_ref[0:1, cols]) * EXP2_SCALE).astype(BF16)
        e_ref[0:rows, cols] = eb
        o_ref[:, cols], stat_ref[1:2, cols] = weigh(vt[:, :rows], eb)
        dp_ref[0:rows, cols] = dot(v[:rows], dot_ref[:, cols], NN)


def gather_block(pieces):
    member = lax.axis_index("head") % GROUP
    odd, high = member % 2 == 1, member // 2 == 1
    if len(pieces) == 2:
        mine, other = pieces[0][...], pieces[1][...]
    else:
        mine, mine_x, other, other_x = [p[...] for p in pieces]
        mine = [jnp.where(high, mine_x, mine), jnp.where(high, mine, mine_x)]
        other = [jnp.where(high, other_x, other), jnp.where(high, other, other_x)]
        mine, other = jnp.concatenate(mine, axis=0), jnp.concatenate(other, axis=0)
    return jnp.where(odd, other, mine), jnp.where(odd, mine, other)


def write_part(send_ref, keep_ref, g_ref, which):
    part = HEAD_DIM // GROUP
    member = lax.axis_index("head") % GROUP
    odd, high = member % 2, member // 2
    for far in range(2):
        x = high if far == 0 else 1 - high
        mine = pl.ds(pl.multiple_of((2 * x + odd) * part, part), part)
        theirs = pl.ds(pl.multiple_of((2 * x + 1 - odd) * part, part), part)
        keep_ref[far, which] = g_ref[which, mine, :]
        send_ref[far, which] = g_ref[which, theirs, :].astype(BF16)


def write_parts(send_ref, keep_ref, g_ref):
    for which in range(2):
        write_part(send_ref, keep_ref, g_ref, which)


def exists(distance):
    return lax.axis_index("ctx") >= distance


def weights_of(k, vt, bias, m, queries_t, s_ref, e_ref, exact):
    if exact:
        s = dot(k[:, :HEAD_DIM], queries_t, NN) + bias
        s_ref[...] = s
        m = jnp.maximum(m, jnp.max(s, axis=0, keepdims=True))
        s = s_ref[...] - m
    else:
        s = dot(k, less(queries_t, m), NN) + bias
    eb = jnp.exp2(s * EXP2_SCALE).astype(BF16)
    e_ref[...] = eb
    o, total = weigh(vt, eb)
    return m, o, total


def twice(run):
    totals = run(False)
    highest = functools.reduce(jnp.maximum, [jnp.max(total) for total in totals])

    @pl.when(jnp.logical_not(highest <= SAFE_SUM))
    def _():
        run(True)


def mask_kernel(tok, doc_ref, near_ref, far_ref):
    tile = tile_of(tok)
    far = far_ref.shape[0]
    for q0 in range(0, tok, tile):
        first = first_visible(doc_ref, q0, tile)
        cols = slice(q0, q0 + tile)
        key = lax.broadcasted_iota(jnp.int32, (tok, tile), 0) - tok
        near_ref[:, cols] = jnp.where(key >= first, 0.0, HIDDEN)
        key = (q0 - far - tok) + lax.broadcasted_iota(jnp.int32, (far - q0, tile), 0)
        far_ref[q0:, cols] = jnp.where(key >= first, 0.0, HIDDEN)


def near_kernel(
    tok, heads, bias_ref, o_own, stat_own, qt_ref, mine_ref, other_ref,
    e_ref, o_ref, stat_ref, k_ref, v_ref, s_ref,
):
    tile = tile_of(tok)

    def run(exact):
        k, v = gather_block((mine_ref, other_ref))
        k_ref[...] = k
        v_ref[...] = v
        k = beside_ones(k)
        vt = with_ones(v.T)
        totals = []
        wide = [bias_ref[:, q0 : q0 + tile] for q0, _, _ in col_blocks(tok, heads)]
        m_own = stat_own[0:1, :]
        m, o, total = weights_of(
            k, vt, jnp.concatenate(wide, axis=1), m_own, qt_ref[...], s_ref, e_ref, exact
        )
        alpha = jnp.exp2((m_own - m) * EXP2_SCALE)
        o_ref[...] = o_own[...] * alpha + o
        stat_ref[0:1, :] = m
        stat_ref[1:2, :] = stat_own[1:2, :] * alpha + total
        totals.append(total)
        return totals

    @pl.when(exists(1))
    def _():
        twice(run)

    @pl.when(jnp.logical_not(exists(1)))
    def _():
        stat_ref[...] = stat_own[...]
        o_ref[...] = o_own[...]


def far_kernel(
    tok, heads, hops, n_kv, bias_ref, stat_own, o_near, stat_near, qt_ref, dot_ref, *refs
):
    pieces, refs = refs[:n_kv], refs[n_kv:]
    send_ref, keep_ref, ds_ref, attn_ref, stat_ref, k_ref, s_ref, e_ref, g_ref = refs
    tile = tile_of(tok)
    far = (hops - 1) * tok
    width = heads * tok
    wide = wide_blocks(tok, heads)

    def finish(cols, m, total, o):
        inverse = 1.0 / total
        attn = (o * inverse).astype(BF16)
        attn_ref[:, cols] = attn
        do_t = dot_ref[:, cols].astype(F32)
        delta = jnp.sum(do_t * attn.astype(F32), axis=0, keepdims=True)
        for row, other in ((0, stat_own), (1, stat_near)):
            stat_ref[row : row + 1, cols] = inverse * jnp.exp2(
                (other[0:1, cols] - m) * EXP2_SCALE
            )
        stat_ref[2:3, cols] = inverse
        stat_ref[3:4, cols] = delta
        return inverse, delta, do_t

    def run(exact):
        blocks = [gather_block(pieces[4 * d - 8 : 4 * d - 4]) for d in range(hops, 1, -1)]
        k = jnp.concatenate([b[0] for b in blocks], axis=0)
        v = jnp.concatenate([b[1] for b in blocks], axis=0)
        k_ref[...] = k
        k = beside_ones(k)
        vt = with_ones(v.T)
        dos, qs, totals = [], [], []
        for q0, cols in wide:
            bias = jnp.concatenate([bias_ref[q0:, q0 : q0 + tile]] * heads, axis=1)
            m_near = stat_near[0:1, cols]
            m, o, total = weights_of(
                k[q0:], vt[:, q0:], bias, m_near, qt_ref[:, cols],
                s_ref.at[q0:, cols], e_ref.at[q0:, cols], exact,
            )
            totals.append(total)
            alpha = jnp.exp2((m_near - m) * EXP2_SCALE)
            total = stat_near[1:2, cols] * alpha + total
            inverse, delta, do_t = finish(cols, m, total, o_near[:, cols] * alpha + o)
            dp = dot(v[q0:], dot_ref[:, cols], NN)
            ds_ref[q0:, cols] = e_ref[q0:, cols] * (dp - delta).astype(BF16)
            dos.append((do_t * inverse).astype(BF16))
            qs.append((qt_ref[:, cols].astype(F32) * (SCALE * inverse)).astype(BF16))
        dos, qs = jnp.concatenate(dos, axis=1), jnp.concatenate(qs, axis=1)
        for r0 in range(0, far, tile):
            rows = slice(r0, r0 + tile)
            c1 = min(width, (r0 // tile + 1) * heads * tile)
            g_ref[1, :, rows] = dot(dos[:, :c1], e_ref[rows, :c1], NT)
            g_ref[0, :, rows] = dot(qs[:, :c1], ds_ref[rows, :c1], NT)
        write_parts(send_ref, keep_ref, g_ref)
        return totals

    @pl.when(exists(2))
    def _():
        twice(run)

    @pl.when(jnp.logical_not(exists(2)))
    def _():
        send_ref[...] = jnp.zeros_like(send_ref)
        keep_ref[...] = jnp.zeros_like(keep_ref)
        for q0, cols in wide:
            finish(cols, stat_near[0:1, cols], stat_near[1:2, cols], o_near[:, cols])


def near_grad_kernel(
    tok, heads, e_ref, v_ref, stat_ref, qt_ref, dot_ref, send_ref, keep_ref, ds_ref, g_ref
):
    tile = tile_of(tok)

    @pl.when(exists(1))
    def _():
        inverse, delta = stat_ref[1:2, :], stat_ref[3:4, :]
        dp = dot(beside_ones(v_ref[...]), less(dot_ref[...], delta), NN)
        ds_ref[...] = e_ref[...] * dp.astype(BF16)
        dos = (dot_ref[...].astype(F32) * inverse).astype(BF16)
        qs = (qt_ref[...].astype(F32) * (SCALE * inverse)).astype(BF16)
        for which, left, right in ((1, dos, e_ref), (0, qs, ds_ref)):
            g_ref[which] = dot(left, right[...], NT)
            write_part(send_ref, keep_ref, g_ref, which)

    @pl.when(jnp.logical_not(exists(1)))
    def _():
        send_ref[...] = jnp.zeros_like(send_ref)
        keep_ref[...] = jnp.zeros_like(keep_ref)


def own_grad_kernel(
    tok, heads, e_ref, dp_ref, stat_ref, qt_ref, dot_ref, send_ref, keep_ref, ds_ref, g_ref
):
    tile = tile_of(tok)
    qs, dos = [], []
    for q0, h, c0 in col_blocks(tok, heads):
        cols = slice(c0, c0 + tile)
        rows = q0 + tile
        inverse, delta = stat_ref[0:1, cols], stat_ref[3:4, cols]
        ds_ref[0:rows, cols] = (
            e_ref[0:rows, cols].astype(F32) * (dp_ref[0:rows, cols] - delta)
        ).astype(BF16)
        dos.append((dot_ref[:, cols].astype(F32) * inverse).astype(BF16))
        qs.append((qt_ref[:, cols].astype(F32) * (SCALE * inverse)).astype(BF16))
    qs, dos = jnp.concatenate(qs, axis=1), jnp.concatenate(dos, axis=1)
    for r0 in range(0, tok, tile):
        rows, c0 = slice(r0, r0 + tile), r0 * heads
        g_ref[1, :, rows] = dot(dos[:, c0:], e_ref[rows, c0:], NT)
        g_ref[0, :, rows] = dot(qs[:, c0:], ds_ref[rows, c0:], NT)
    write_parts(send_ref, keep_ref, g_ref)


def query_kernel(
    tok, heads, hops, kt_own, k_near, k_far, ds_far, ds_near, ds_own, attn_ref, stat_ref,
    out_ref, qgrad_ref, sum_ref,
):
    tile = tile_of(tok)
    blocks = col_blocks(tok, heads)
    for q0, h, c0 in blocks:
        cols = slice(c0, c0 + tile)
        rows = q0 + tile
        out_ref[place_of(q0, h, tile)] = attn_ref[:, cols].T
        sum_ref[:, cols] = dot(kt_own[:, :rows], ds_own[0:rows, cols], NN) * stat_ref[0:1, cols]

    @pl.when(exists(1))
    def _():
        kt = k_near[...].T
        for q0, h, c0 in blocks:
            cols = slice(c0, c0 + tile)
            sum_ref[:, cols] += dot(kt, ds_near[:, cols], NN) * stat_ref[1:2, cols]

    @pl.when(exists(2))
    def _():
        kt = k_far[...].T
        for q0, h, c0 in blocks:
            cols = slice(c0, c0 + tile)
            sum_ref[:, cols] += dot(kt[:, q0:], ds_far[q0:, cols], NN) * stat_ref[2:3, cols]

    for q0, h, c0 in blocks:
        grad = sum_ref[:, c0 : c0 + tile] * SCALE
        qgrad_ref[place_of(q0, h, tile)] = grad.T.astype(BF16)


def sum_kernel(own_ref, *refs):
    for which, out_ref in enumerate(refs[-2:]):
        total = own_ref[0, which]
        for ref in refs[:-2]:
            total += ref[which].astype(F32)
        out_ref[...] = total


def call(kernel, shapes, operands, scratch=(), flops=0, limit=24):
    size = sum(math.prod(s.shape) * s.dtype.itemsize for s in shapes)
    size += sum(o.size * o.dtype.itemsize for o in operands)
    return pl.pallas_call(
        kernel,
        out_shape=shapes,
        in_specs=[pl.BlockSpec(memory_space=pltpu.VMEM)] * len(operands),
        out_specs=[pl.BlockSpec(memory_space=pltpu.VMEM)] * len(shapes),
        scratch_shapes=list(scratch),
        compiler_params=pltpu.CompilerParams(vmem_limit_bytes=limit << 20),
        cost_estimate=pl.CostEstimate(flops=flops, bytes_accessed=size, transcendentals=0),
    )(*operands)


def shift(array, step):
    size = lax.axis_size("ctx")
    route = [(c, c + step) for c in range(size) if 0 <= c + step < size]
    return lax.ppermute(array, "ctx", route)


def swap(array, stride):
    return lax.ppermute(array, "head", [(i, i ^ stride) for i in range(lax.axis_size("head"))])


def together(*arrays):
    return lax.optimization_barrier(arrays)


def body(queries, keys, values, out_grad, doc_start):
    tok, q_width = queries.shape
    heads = q_width // HEAD_DIM
    hops = WINDOW // tok
    reach = hops * tok
    far = reach - tok
    width = heads * tok
    part = HEAD_DIM // GROUP
    shape = jax.ShapeDtypeStruct
    everywhere = pl.BlockSpec(memory_space=pltpu.HBM)
    half, quarter = pl.pallas_call(
        pack_kernel,
        out_shape=[shape((tok, HEAD_DIM), BF16), shape((tok // 2, HEAD_DIM), BF16)],
        in_specs=[everywhere] * 2,
        out_specs=[pl.BlockSpec(memory_space=pltpu.VMEM)] * 2,
        scratch_shapes=[pltpu.SemaphoreType.DMA((2,))],
        compiler_params=pltpu.CompilerParams(vmem_limit_bytes=55040 << 10),
    )(keys, values)
    half = pl.pallas_call(
        late_pack_kernel,
        out_shape=shape((tok, HEAD_DIM), BF16),
        in_specs=[everywhere] * 2 + [pl.BlockSpec(memory_space=pltpu.VMEM)],
        out_specs=pl.BlockSpec(memory_space=pltpu.VMEM),
        scratch_shapes=[pltpu.SemaphoreType.DMA],
        input_output_aliases={2: 0},
        compiler_params=pltpu.CompilerParams(vmem_limit_bytes=55040 << 10),
    )(keys, values, half)
    came = [shift(quarter if d > 1 else half, d) for d in range(hops, 0, -1)][::-1]
    doc = doc_start.reshape(1, tok)
    causal = call(
        causal_kernel,
        [shape((tile_of(tok), tile_of(tok)), F32)],
        [],
        flops=64 * tok * tok * HEAD_DIM,
    )[0]
    causal, *tied = together(causal, *came[1:])
    came = [came[0], *tied]
    e_own, dp_own, o_own, stat_own, q_t, do_t, kt_own = call(
        functools.partial(own_kernel, tok, heads),
        [
            shape((tok, width), BF16),
            shape((tok, width), F32),
            shape((HEAD_DIM, width), F32),
            shape((2, width), F32),
            shape((HEAD_DIM, width), BF16),
            shape((HEAD_DIM, width), BF16),
            shape((HEAD_DIM, tok), BF16),
        ],
        [causal, doc, queries, keys, out_grad, values],
        scratch=[pltpu.VMEM((tok, width), F32)],
        flops=6 * tok * width * HEAD_DIM,
    )
    near, stat_own = together(came[0], stat_own)
    near = [near, swap(near, 1)]
    pieces = []
    for block in came[1:]:
        across = swap(block, 2)
        pieces += [block, across, swap(block, 1), swap(across, 1)]
    _, doc = together(stat_own, doc)
    near_bias, far_bias = call(
        functools.partial(mask_kernel, tok),
        [shape((tok, tok), F32), shape((far, tok), F32)],
        [doc],
        flops=64 * tok * tok * HEAD_DIM,
    )
    e_near, o_near, stat_near, k_near, v_near = call(
        functools.partial(near_kernel, tok, heads),
        [
            shape((tok, width), BF16),
            shape((HEAD_DIM, width), F32),
            shape((2, width), F32),
            shape((tok, HEAD_DIM), BF16),
            shape((tok, HEAD_DIM), BF16),
        ],
        [near_bias, o_own, stat_own, q_t, *near],
        scratch=[pltpu.VMEM((tok, width), F32)],
        flops=6 * tok * width * HEAD_DIM,
    )
    send_far, keep_far, ds_far, attn_t, stat, k_far = call(
        functools.partial(far_kernel, tok, heads, hops, len(pieces)),
        [
            shape((2, 2, part, far), BF16),
            shape((2, 2, part, far), F32),
            shape((far, width), BF16),
            shape((HEAD_DIM, width), BF16),
            shape((4, width), F32),
            shape((far, HEAD_DIM), BF16),
        ],
        [far_bias, stat_own, o_near, stat_near, q_t, do_t, *pieces],
        scratch=[
            pltpu.VMEM((far, width), F32),
            pltpu.VMEM((far, width), BF16),
            pltpu.VMEM((2, HEAD_DIM, far), F32),
        ],
        flops=10 * far * width * HEAD_DIM,
    )
    gradients = [
        shape((2, 2, part, tok), BF16),
        shape((2, 2, part, tok), F32),
        shape((tok, width), BF16),
    ]
    send_near, keep_near, ds_near = call(
        functools.partial(near_grad_kernel, tok, heads),
        gradients,
        [e_near, v_near, stat, q_t, do_t],
        scratch=[pltpu.VMEM((2, HEAD_DIM, tok), F32)],
        flops=6 * tok * width * HEAD_DIM,
    )
    pair_far = keep_far + swap(send_far, 1).astype(F32)
    whole = (pair_far[0] + swap(pair_far[1].astype(BF16), 2).astype(F32)).astype(BF16)
    pair_near = keep_near + swap(send_near, 1).astype(F32)
    pair_near, stat_late = together(pair_near, stat)
    near = (pair_near[0] + swap(pair_near[1].astype(BF16), 2).astype(F32)).astype(BF16)
    send_own, keep_own, ds_own = call(
        functools.partial(own_grad_kernel, tok, heads),
        gradients,
        [e_own, dp_own, stat_late, q_t, do_t],
        scratch=[pltpu.VMEM((2, HEAD_DIM, tok), F32)],
        flops=4 * tok * width * HEAD_DIM,
    )
    attn_out, query_grad = call(
        functools.partial(query_kernel, tok, heads, hops),
        [shape((tok, q_width), BF16)] * 2,
        [kt_own, k_near, k_far, ds_far, ds_near, ds_own, attn_t, stat],
        scratch=[pltpu.VMEM((HEAD_DIM, width), F32)],
        flops=2 * (reach + tok) * width * HEAD_DIM,
    )
    pair_own = keep_own + swap(send_own, 1).astype(F32)
    near, crossing = together(near, pair_own[1].astype(BF16))
    returned = [
        shift(whole[:, :, (hops - d) * tok : (hops - d + 1) * tok], -d) for d in range(hops, 1, -1)
    ]
    returned += [shift(near, -1), swap(crossing, 2)]
    key_grad, value_grad = call(
        sum_kernel, [shape((part, tok), F32)] * 2, [pair_own, *returned], limit=16
    )
    return attn_out, query_grad, key_grad.T, value_grad.T


def solution(mesh):
    placed = (P("ctx", "head"), P("ctx", None), P("ctx", None), P("ctx", "head"), P("ctx"))
    return jax.shard_map(
        body,
        mesh=mesh,
        in_specs=placed,
        out_specs=(P("ctx", "head"),) * 4,
        check_vma=False,
    )
```
